32 devices in a mesh: group: 2 (over y), blk: 16 (over z, x, core).
Axes of the slice: x: 2, y: 2, z: 4, core: 2. Of those that a mesh axis runs over, the one named last changes fastest.
Arguments:
- student_hidden: bfloat16 [64, 4096], P(('group', 'blk')), parts along dimension 0, may hold values from -512 to 512
- teacher_hidden: bfloat16 [64, 1, 5120], P(('group', 'blk')), parts along dimension 0, may hold values from -512 to 512
- counts: int32 [64], P(('group', 'blk')), parts along dimension 0, may hold values from 0 to 7
- student_head: bfloat16 [8192, 10240], P('group', 'blk'), parts along dimension 0, may hold values from -16 to 16
- teacher_head: bfloat16 [1, 10240, 10240], P(None, 'group', 'blk'), parts along dimension 1, may hold values from -16 to 16
Outputs:
- row_loss: float32 [64], P(('group', 'blk')), parts along dimension 0
- grad_hidden: bfloat16 [64, 4096], P(('group', 'blk')), parts along dimension 0
The draws below stay inside these ranges and needn't reach their ends.
There are 2 independent parts, one for each index of `group`. The reference program is written for one: setup_inputs(seed, part) draws one part's arguments, and reference() takes and returns one part's arrays. A program takes and returns all parts, laid end to end along the dimension named above; each array names one. Nothing has to cross between parts.
All inputs are finite; a program needn't handle non-finite values.
Results may differ from the reference program's by a relative error of at most 0.0046.
Values may be sent and summed in bfloat16 or wider, within the bound.
A program may use at most 64 MiB of HBM per device.

```python
import math
import jax
import jax.numpy as jnp
from jax import lax

DS = 4096
DT = 5120
TEACH = 1
ROWS = 32
VOCAB = 10240


def head_parts(key, salt, width, number):
    key = jax.random.fold_in(key, salt)
    first_key, second_key = jax.random.split(key, 2)
    normal_part = jnp.clip(jax.random.normal(first_key, (number, width, VOCAB), jnp.float32), -6.0, 6.0)
    column_scale = jnp.exp(jax.random.uniform(second_key, (number, 1, VOCAB), jnp.float32, 0.0, math.log(10.0)))
    return normal_part * column_scale / math.sqrt(width)


def row_scales(key, shape, lowest, highest):
    return jnp.exp(jax.random.uniform(key, shape, jnp.float32, math.log(lowest), math.log(highest)))


def draw_student_head(key, part):
    weights = head_parts(key, 11, DS, 1)
    return weights[0].astype(jnp.bfloat16)


def draw_teacher_head(key, part):
    weights = head_parts(key, 12, DT, TEACH)
    return weights.astype(jnp.bfloat16)


def draw_student_hidden(key, part):
    lowest = 0.005
    highest = 0.3
    key = jax.random.fold_in(key, 21)
    hidden = jax.random.normal(key, (ROWS, 1, DS), jnp.float32)
    hidden = hidden * row_scales(jax.random.fold_in(key, 22), (ROWS, 1, 1), lowest, highest)
    return hidden[:, 0, :].astype(jnp.bfloat16)


def draw_teacher_hidden(key, part):
    lowest = 0.03
    highest = 0.3
    key = jax.random.fold_in(key, 23)
    hidden = jax.random.normal(key, (ROWS, TEACH, DT), jnp.float32)
    hidden = hidden * row_scales(jax.random.fold_in(key, 24), (ROWS, 1, 1), lowest, highest)
    return hidden.astype(jnp.bfloat16)


def draw_counts(key, part):
    key = jax.random.fold_in(key, 31)
    limits = 2 + 6 * jnp.arange(ROWS, dtype=jnp.int32) // ROWS
    values = jax.random.randint(key, (ROWS,), 0, limits, dtype=jnp.int32)
    return values.at[0].set(0).at[ROWS - 1].set(7)


def setup_inputs(seed: int = 0, part: int = 0) -> dict:
    splits = jax.random.split(jax.random.key(seed), 6)
    own_keys = jax.random.split(jax.random.fold_in(splits[5], part), 6)
    student_hidden = draw_student_hidden(jax.random.fold_in(jax.random.fold_in(splits[5], part), 71), part)
    teacher_hidden = draw_teacher_hidden(jax.random.fold_in(jax.random.fold_in(splits[5], part), 71), part)
    counts = draw_counts(jax.random.fold_in(jax.random.fold_in(splits[5], part), 71), part)
    student_head = draw_student_head(jax.random.fold_in(jax.random.fold_in(splits[5], part), 71), part)
    teacher_head = draw_teacher_head(jax.random.fold_in(jax.random.fold_in(splits[5], part), 71), part)
    return {"student_hidden": student_hidden, "teacher_hidden": teacher_hidden, "counts": counts, "student_head": student_head, "teacher_head": teacher_head}


def reference(student_hidden, teacher_hidden, counts, student_head, teacher_head):
    student_logit = jnp.dot(student_hidden, student_head, preferred_element_type=jnp.float32)
    poe_score = jnp.zeros_like(student_logit)
    for teacher in range(TEACH):
        poe_score = poe_score + jnp.dot(teacher_hidden[:, teacher, :], teacher_head[teacher], preferred_element_type=jnp.float32)
    poe_score = poe_score / TEACH
    total_count = jnp.sum(counts).astype(jnp.float32)
    omega = counts.astype(jnp.float32) * ROWS / total_count
    peak_student = jnp.max(student_logit, axis=1, keepdims=True)
    lse_student = peak_student[:, 0] + jnp.log(jnp.sum(jnp.exp(student_logit - peak_student), axis=1))
    peak_poe = jnp.max(poe_score, axis=1, keepdims=True)
    lse_poe = peak_poe[:, 0] + jnp.log(jnp.sum(jnp.exp(poe_score - peak_poe), axis=1))
    poe_prob = jnp.exp(poe_score - lse_poe[:, None])
    student_prob = jnp.exp(student_logit - lse_student[:, None])
    divergence = jnp.sum(poe_prob * (poe_score - student_logit), axis=1) - lse_poe + lse_student
    row_loss = omega * divergence
    coeff = (student_prob - poe_prob).astype(jnp.bfloat16)
    partial_value = lax.dot_general(coeff, student_head, (((1,), (1,)), ((), ())), preferred_element_type=jnp.float32)
    grad_hidden = (partial_value * omega[:, None]).astype(jnp.bfloat16)
    return row_loss, grad_hidden
```

```python
import functools

import jax
import jax.numpy as jnp
from jax import lax
from jax.experimental import pallas as pl
from jax.experimental.pallas import tpu as pltpu
from jax.sharding import PartitionSpec as P

MESH = pl.DeviceIdType.MESH
F32 = jnp.float32
BF16 = jnp.bfloat16
CUTS = 2


def kernel(
    n, far, counts_ref, sh_ref, th_ref, sw_ref, tw_ref, loss_ref, grad_ref,
    sheld, theld, xs, xt, sw, tw, part, outbox, inbox, stats, table,
    w_sem, send_sem, recv_sem, stat_send, stat_recv, part_send, part_recv,
):
    row_dev, ds = sh_ref.shape
    dt = th_ref.shape[1]
    rows = n * row_dev
    near = n // (2 * far)
    me = lax.axis_index("blk")
    core = lax.rem(me, 2)
    b = lax.rem(me // 2, near)
    a = me // (2 * near)
    wide = ds // CUTS

    def index(da, db, dc):
        return (
            lax.rem(a + da + far, far) * near + lax.rem(b + db + near, near)
        ) * 2 + lax.rem(core + dc, 2)

    weights = []
    for which, (src, dst) in enumerate(((sw_ref, sw), (tw_ref, tw))):
        step = src.shape[0] // 4
        for k in range(4):
            copy = pltpu.make_async_copy(
                src.at[pl.ds(k * step, step)], dst.at[pl.ds(k * step, step)], w_sem.at[which, k]
            )
            copy.start()
            weights.append(copy)

    barrier = pltpu.get_barrier_semaphore()

    def greet(k, carry):
        pl.semaphore_signal(
            barrier, inc=1, device_id={"blk": lax.rem(me + k, n)}, device_id_type=MESH
        )
        return carry

    lax.fori_loop(1, n, greet, 0)
    pl.semaphore_wait(barrier, n - 1)

    sends = []
    used = [0, 0]

    def send(which, src, slot, target):
        held = (sheld, theld)[which]
        copy = pltpu.make_async_remote_copy(
            src_ref=src,
            dst_ref=held.at[slot],
            send_sem=send_sem.at[which, used[which]],
            recv_sem=recv_sem.at[which, slot],
            device_id={"blk": target},
            device_id_type=MESH,
        )
        used[which] += 1
        copy.start()
        sends.append(copy)

    def arrive(which, slot):
        held = (sheld, theld)[which]
        pltpu.make_async_remote_copy(
            src_ref=held.at[slot],
            dst_ref=held.at[slot],
            send_sem=send_sem.at[which, 0],
            recv_sem=recv_sem.at[which, slot],
            device_id={"blk": me},
            device_id_type=MESH,
        ).wait_recv()

    for which, own in enumerate((sh_ref, th_ref)):
        for da in range(1, far):
            send(which, own, me, index(da, 0, 0))
        for db in range(1, near):
            send(which, own, me, index(0, db, 0))
        send(which, own, me, index(0, 0, 1))
    for which, own in enumerate((sh_ref, th_ref)):
        for da in range(1, far):
            slot = index(-da, 0, 0)
            arrive(which, slot)
            held = (sheld, theld)[which].at[slot]
            for db in range(1, near):
                send(which, held, slot, index(0, db, 0))
            send(which, held, slot, index(0, 0, 1))
        for db in range(1, near):
            for da in range(far):
                slot = index(-da, -db, 0)
                arrive(which, slot)
                send(which, (sheld, theld)[which].at[slot], slot, index(0, 0, 1))

    def product(which, x, w, width):
        held = (sheld, theld)[which]
        own = (sh_ref, th_ref)[which]
        for db in range(near):
            for da in range(far):
                arrive(which, index(-da, -db, 1))
        held[me] = own[...]
        for d in range(n):
            x[pl.ds(d * row_dev, row_dev), :] = held[d].astype(F32)
        for copy in weights[4 * which:4 * which + 4]:
            copy.wait()
        cut = width // 8

        def body(k, total):
            at = pl.ds(pl.multiple_of(k * cut, cut), cut)
            return total + jnp.dot(
                x[:, at].astype(BF16), w[at, :], preferred_element_type=F32
            )

        return lax.fori_loop(0, 8, body, jnp.zeros((rows, w.shape[1]), F32))

    student = product(0, xs, sw, ds)
    score = product(1, xt, tw, dt)

    peak_s = jnp.max(student, axis=1, keepdims=True)
    peak_p = jnp.max(score, axis=1, keepdims=True)
    exp_p = jnp.exp(score - peak_p)
    sum_s = jnp.sum(jnp.exp(student - peak_s), axis=1, keepdims=True)
    sum_p = jnp.sum(exp_p, axis=1, keepdims=True)
    weighted = jnp.sum(exp_p * (score - student), axis=1, keepdims=True)
    own_count = counts_ref[0]
    for r in range(1, row_dev):
        own_count = own_count + counts_ref[r]
    padded = table.shape[0]
    lane = lax.broadcasted_iota(jnp.int32, (rows, 128), 1)
    packed = jnp.where(lane == 5, own_count.astype(F32), 0.0)
    for k, column in enumerate((peak_s, sum_s, peak_p, sum_p, weighted)):
        packed = jnp.where(lane == k, column, packed)
    table[pl.ds(0, rows), :] = packed
    if padded > rows:
        table[pl.ds(rows, padded - rows), :] = jnp.zeros((padded - rows, 128), F32)
    stats[me] = jnp.transpose(table[...])[:8, :]

    def stat_copy(k):
        return pltpu.make_async_remote_copy(
            src_ref=stats.at[me],
            dst_ref=stats.at[me],
            send_sem=stat_send.at[k],
            recv_sem=stat_recv.at[me],
            device_id={"blk": lax.rem(me + k, n)},
            device_id_type=MESH,
        )

    def stat_start(k, carry):
        stat_copy(k).start()
        return carry

    def stat_wait(k, carry):
        slot = lax.rem(me + k, n)
        pltpu.make_async_remote_copy(
            src_ref=stats.at[slot],
            dst_ref=stats.at[slot],
            send_sem=stat_send.at[k],
            recv_sem=stat_recv.at[slot],
            device_id={"blk": me},
            device_id_type=MESH,
        ).wait_recv()
        return carry

    lax.fori_loop(1, n, stat_start, 0)
    lax.fori_loop(1, n, stat_wait, 0)

    all_stats = stats[...]
    top_s = jnp.max(all_stats[:, 0:1, :], axis=0)
    top_p = jnp.max(all_stats[:, 2:3, :], axis=0)
    scale_p = jnp.exp(all_stats[:, 2:3, :] - top_p[None])
    total_s = jnp.sum(jnp.exp(all_stats[:, 0:1, :] - top_s[None]) * all_stats[:, 1:2, :], axis=0)
    total_p = jnp.sum(scale_p * all_stats[:, 3:4, :], axis=0)
    total_w = jnp.sum(scale_p * all_stats[:, 4:5, :], axis=0)
    total_count = jnp.sum(all_stats[:, 5:6, :], axis=0)
    lse_s = top_s + jnp.log(total_s)
    lse_p = top_p + jnp.log(total_p)
    divergence = total_w / total_p - lse_p + lse_s
    line = lax.broadcasted_iota(jnp.int32, (128, padded), 0)
    merged = jnp.where(line == 0, lse_s, 0.0)
    merged = jnp.where(line == 1, lse_p, merged)
    merged = jnp.where(line == 2, divergence, merged)
    merged = jnp.where(line == 3, total_count, merged)
    table[...] = jnp.transpose(merged)

    coeff = (
        jnp.exp(student - table[pl.ds(0, rows), 0:1]) - jnp.exp(score - table[pl.ds(0, rows), 1:2])
    ).astype(BF16)

    own_rows = table[pl.ds(me * row_dev, row_dev), :]
    row = lax.broadcasted_iota(jnp.int32, (row_dev, 1), 0)
    own_counts = jnp.zeros((row_dev, 1), F32)
    for r in range(row_dev):
        own_counts = jnp.where(row == r, counts_ref[r].astype(F32), own_counts)
    omega = own_counts * rows / own_rows[:, 3:4]
    loss_ref[...] = jnp.broadcast_to(omega * own_rows[:, 2:3], loss_ref.shape)

    def part_copy(h, k):
        target = lax.rem(me + k, n)
        return pltpu.make_async_remote_copy(
            src_ref=outbox.at[h, target],
            dst_ref=inbox.at[h, me],
            send_sem=part_send.at[h, k],
            recv_sem=part_recv.at[h, me],
            device_id={"blk": target},
            device_id_type=MESH,
        )

    strip = 512 if wide % 512 == 0 else wide
    for h in range(CUTS):

        def grad_body(k, carry, h=h):
            at = pl.ds(pl.multiple_of(k * strip, strip), strip)
            wat = pl.ds(pl.multiple_of(h * wide + k * strip, strip), strip)
            part[:, at] = lax.dot_general(
                coeff, sw[wat, :], (((1,), (1,)), ((), ())), preferred_element_type=F32
            )
            return carry

        lax.fori_loop(0, wide // strip, grad_body, 0)
        for d in range(n):
            outbox[h, d] = part[pl.ds(d * row_dev, row_dev), :].astype(BF16)
        inbox[h, me] = outbox[h, me]

        def part_start(k, carry, h=h):
            part_copy(h, k).start()
            return carry

        lax.fori_loop(1, n, part_start, 0)

    for h in range(CUTS):

        def part_wait(k, carry, h=h):
            slot = lax.rem(me + k, n)
            pltpu.make_async_remote_copy(
                src_ref=inbox.at[h, slot],
                dst_ref=inbox.at[h, slot],
                send_sem=part_send.at[h, k],
                recv_sem=part_recv.at[h, slot],
                device_id={"blk": me},
                device_id_type=MESH,
            ).wait_recv()
            return carry

        lax.fori_loop(1, n, part_wait, 0)
        total = jnp.zeros((row_dev, wide), F32)
        for d in range(n):
            total = total + inbox[h, d].astype(F32)
        grad_ref[:, pl.ds(h * wide, wide)] = (total * omega).astype(BF16)

    for copy in sends:
        copy.wait_send()

    def drain(k, carry):
        stat_copy(k).wait_send()
        for h in range(CUTS):
            part_copy(h, k).wait_send()
        return carry

    lax.fori_loop(1, n, drain, 0)


def on_device(n, student_hidden, teacher_hidden, counts, student_head, teacher_head):
    row_dev, ds = student_hidden.shape
    dt = teacher_hidden.shape[2]
    vocab = student_head.shape[1]
    rows = n * row_dev
    padded = -(-rows // 128) * 128
    far = 4 if (n // 2) % 4 == 0 else 1
    wide = ds // CUTS
    loss, grad = pl.pallas_call(
        functools.partial(kernel, n, far),
        out_shape=(
            jax.ShapeDtypeStruct((row_dev, 128), F32),
            jax.ShapeDtypeStruct((row_dev, ds), BF16),
        ),
        in_specs=[
            pl.BlockSpec(memory_space=pltpu.SMEM),
            pl.BlockSpec(memory_space=pltpu.VMEM),
            pl.BlockSpec(memory_space=pltpu.VMEM),
            pl.BlockSpec(memory_space=pl.ANY),
            pl.BlockSpec(memory_space=pl.ANY),
        ],
        out_specs=(
            pl.BlockSpec(memory_space=pltpu.VMEM),
            pl.BlockSpec(memory_space=pltpu.VMEM),
        ),
        scratch_shapes=[
            pltpu.VMEM((n, row_dev, ds), BF16),
            pltpu.VMEM((n, row_dev, dt), BF16),
            pltpu.VMEM((rows, ds), F32),
            pltpu.VMEM((rows, dt), F32),
            pltpu.VMEM((ds, vocab), BF16),
            pltpu.VMEM((dt, vocab), BF16),
            pltpu.VMEM((rows, wide), F32),
            pltpu.VMEM((CUTS, n, row_dev, wide), BF16),
            pltpu.VMEM((CUTS, n, row_dev, wide), BF16),
            pltpu.VMEM((n, 8, padded), F32),
            pltpu.VMEM((padded, 128), F32),
            pltpu.SemaphoreType.DMA((2, 4)),
            pltpu.SemaphoreType.DMA((2, n)),
            pltpu.SemaphoreType.DMA((2, n)),
            pltpu.SemaphoreType.DMA((n,)),
            pltpu.SemaphoreType.DMA((n,)),
            pltpu.SemaphoreType.DMA((CUTS, n)),
            pltpu.SemaphoreType.DMA((CUTS, n)),
        ],
        compiler_params=pltpu.CompilerParams(
            collective_id=0, has_side_effects=True, vmem_limit_bytes=56 * 1024 * 1024
        ),
    )(counts, student_hidden, teacher_hidden.reshape(row_dev, dt), student_head, teacher_head.reshape(dt, vocab))
    return loss[:, 0], grad


def solution(mesh):
    return jax.shard_map(
        functools.partial(on_device, mesh.shape["blk"]),
        mesh=mesh,
        in_specs=(
            P(("group", "blk"), None),
            P(("group", "blk"), None, None),
            P(("group", "blk")),
            P("group", "blk"),
            P(None, "group", "blk"),
        ),
        out_specs=(P(("group", "blk")), P(("group", "blk"), None)),
        check_vma=False,
    )
```

```python
import functools

import jax
import jax.numpy as jnp
from jax import lax
from jax.experimental import pallas as pl
from jax.experimental.pallas import tpu as pltpu
from jax.sharding import PartitionSpec as P

MESH = pl.DeviceIdType.MESH
F32 = jnp.float32
BF16 = jnp.bfloat16
CUTS = 2
STEPS = 8


def kernel(
    n, counts_ref, sh_ref, th_ref, sw_ref, tw_ref, loss_ref, grad_ref,
    sheld, theld, xs, xt, sw, tw, part, core_in, outbox, inbox, stats, table,
    w_sem, send_sem, recv_sem, pair_send, pair_recv, stat_send, stat_recv,
    core_send, core_recv, part_send, part_recv,
):
    row_dev, ds = sh_ref.shape
    dt = th_ref.shape[1]
    rows = n * row_dev
    half = rows // 2
    chips = n // 2
    me = lax.axis_index("blk")
    core = lax.rem(me, 2)
    chip = me // 2
    other = me + 1 - 2 * core
    wide = ds // CUTS

    weights = []
    for which, (src, dst) in enumerate(((sw_ref, sw), (tw_ref, tw))):
        copy = pltpu.make_async_copy(src, dst, w_sem.at[which])
        copy.start()
        weights.append(copy)

    barrier = pltpu.get_barrier_semaphore()

    def greet(k, carry):
        pl.semaphore_signal(
            barrier, inc=1, device_id={"blk": lax.rem(me + k, n)}, device_id_type=MESH
        )
        return carry

    lax.fori_loop(1, n, greet, 0)
    pl.semaphore_wait(barrier, n - 1)

    owns = (sh_ref, th_ref)
    helds = (sheld, theld)

    def own_copy(which, k):
        return pltpu.make_async_remote_copy(
            src_ref=owns[which],
            dst_ref=helds[which].at[core, chip],
            send_sem=send_sem.at[which, k],
            recv_sem=recv_sem.at[which, chip],
            device_id={"blk": lax.rem(chip + k, chips) * 2 + core},
            device_id_type=MESH,
        )

    def pair_copy(which, k):
        slot = lax.rem(chip - k + chips, chips)
        return pltpu.make_async_remote_copy(
            src_ref=owns[which] if isinstance(k, int) and k == 0 else helds[which].at[core, slot],
            dst_ref=helds[which].at[core, slot],
            send_sem=pair_send.at[which, slot],
            recv_sem=pair_recv.at[which, slot],
            device_id={"blk": other},
            device_id_type=MESH,
        )

    def landed(which, k):
        slot = lax.rem(chip - k + chips, chips)
        pltpu.make_async_remote_copy(
            src_ref=helds[which].at[core, slot],
            dst_ref=helds[which].at[core, slot],
            send_sem=send_sem.at[which, 0],
            recv_sem=recv_sem.at[which, slot],
            device_id={"blk": other},
            device_id_type=MESH,
        ).wait_recv()

    def pair_landed(which, k):
        slot = lax.rem(chip - k + chips, chips)
        pltpu.make_async_remote_copy(
            src_ref=helds[which].at[1 - core, slot],
            dst_ref=helds[which].at[1 - core, slot],
            send_sem=send_sem.at[which, 0],
            recv_sem=pair_recv.at[which, slot],
            device_id={"blk": other},
            device_id_type=MESH,
        ).wait_recv()

    def loop(low, high, body):
        if high - low <= 16:
            for k in range(low, high):
                body(k)
        else:
            lax.fori_loop(low, high, lambda k, carry: (body(k), carry)[1], 0)

    for which in range(2):
        loop(1, chips, lambda k, which=which: own_copy(which, k).start())
        pair_copy(which, 0).start()

    def pass_on(which, k):
        landed(which, k)
        pair_copy(which, k).start()

    def settle(which, x):
        loop(0, chips, lambda k: pair_landed(which, k))
        for c in range(2):
            for d in range(chips):
                x[pl.ds(c * half + d * row_dev, row_dev), :] = helds[which][c, d].astype(F32)

    def term(x, w, k, total):
        cut = w.shape[0] // STEPS
        at = pl.ds(k * cut, cut)
        return total + jnp.dot(x[:, at].astype(BF16), w[at, :], preferred_element_type=F32)

    sheld[core, chip] = sh_ref[...]
    theld[core, chip] = th_ref[...]
    loop(1, chips, lambda k: pass_on(0, k))
    settle(0, xs)
    weights[0].wait()
    student = jnp.zeros((rows, sw.shape[1]), F32)
    share = -(-(chips - 1) // STEPS)
    for k in range(STEPS):
        student = term(xs, sw, k, student)
        loop(
            1 + k * share, max(1 + k * share, min(chips, 1 + (k + 1) * share)),
            lambda j: pass_on(1, j),
        )
    peak_s = jnp.max(student, axis=1, keepdims=True)
    exp_s = jnp.exp(student - peak_s)
    sum_s = jnp.sum(exp_s, axis=1, keepdims=True)
    settle(1, xt)
    weights[1].wait()
    score = jnp.zeros((rows, tw.shape[1]), F32)
    for k in range(STEPS):
        score = term(xt, tw, k, score)

    peak_p = jnp.max(score, axis=1, keepdims=True)
    exp_p = jnp.exp(score - peak_p)
    sum_p = jnp.sum(exp_p, axis=1, keepdims=True)
    weighted = jnp.sum(exp_p * (score - student), axis=1, keepdims=True)
    own_count = counts_ref[0]
    for r in range(1, row_dev):
        own_count = own_count + counts_ref[r]
    padded = table.shape[0]
    lane = lax.broadcasted_iota(jnp.int32, (rows, 128), 1)
    packed = jnp.where(lane == 5, own_count.astype(F32), 0.0)
    for k, column in enumerate((peak_s, sum_s, peak_p, sum_p, weighted)):
        packed = jnp.where(lane == k, column, packed)
    table[pl.ds(0, rows), :] = packed
    if padded > rows:
        table[pl.ds(rows, padded - rows), :] = jnp.zeros((padded - rows, 128), F32)
    stats[me] = jnp.transpose(table[...])[:8, :]

    def stat_copy(k):
        return pltpu.make_async_remote_copy(
            src_ref=stats.at[me],
            dst_ref=stats.at[me],
            send_sem=stat_send.at[k],
            recv_sem=stat_recv.at[me],
            device_id={"blk": lax.rem(me + k, n)},
            device_id_type=MESH,
        )

    def stat_landed(k):
        slot = lax.rem(me + k, n)
        pltpu.make_async_remote_copy(
            src_ref=stats.at[slot],
            dst_ref=stats.at[slot],
            send_sem=stat_send.at[k],
            recv_sem=stat_recv.at[slot],
            device_id={"blk": other},
            device_id_type=MESH,
        ).wait_recv()

    loop(1, n, lambda k: stat_copy(k).start())

    high_s = exp_s.astype(BF16)
    high_p = exp_p.astype(BF16)
    low_s = (exp_s - high_s.astype(F32)).astype(BF16)
    low_p = (exp_p - high_p.astype(F32)).astype(BF16)
    stacked = jnp.concatenate([high_s, low_s, high_p, low_p], axis=0)
    strip = 512 if wide % 512 == 0 else wide

    def raw(h, k):
        return lax.dot_general(
            stacked, sw[pl.ds(h * wide + k * strip, strip), :], (((1,), (1,)), ((), ())),
            preferred_element_type=F32,
        )

    def scaled(value, scale_s, scale_p):
        return scale_s * (value[:rows] + value[rows:2 * rows]) - scale_p * (
            value[2 * rows:3 * rows] + value[3 * rows:]
        )

    early = [raw(0, k) for k in range(wide // strip)]
    loop(1, n, stat_landed)

    all_stats = stats[...]
    top_s = jnp.max(all_stats[:, 0:1, :], axis=0)
    top_p = jnp.max(all_stats[:, 2:3, :], axis=0)
    change_p = jnp.exp(all_stats[:, 2:3, :] - top_p[None])
    total_s = jnp.sum(jnp.exp(all_stats[:, 0:1, :] - top_s[None]) * all_stats[:, 1:2, :], axis=0)
    total_p = jnp.sum(change_p * all_stats[:, 3:4, :], axis=0)
    total_w = jnp.sum(change_p * all_stats[:, 4:5, :], axis=0)
    total_count = jnp.sum(all_stats[:, 5:6, :], axis=0)
    lse_s = top_s + jnp.log(total_s)
    lse_p = top_p + jnp.log(total_p)
    divergence = total_w / total_p - lse_p + lse_s
    line = lax.broadcasted_iota(jnp.int32, (128, padded), 0)
    merged = jnp.where(line == 0, lse_s, 0.0)
    merged = jnp.where(line == 1, lse_p, merged)
    merged = jnp.where(line == 2, divergence, merged)
    merged = jnp.where(line == 3, total_count, merged)
    table[...] = jnp.transpose(merged)
    scale_s = jnp.exp(peak_s - table[pl.ds(0, rows), 0:1])
    scale_p = jnp.exp(peak_p - table[pl.ds(0, rows), 1:2])

    own_rows = table[pl.ds(core * half + chip * row_dev, row_dev), :]
    row = lax.broadcasted_iota(jnp.int32, (row_dev, 1), 0)
    own_counts = jnp.zeros((row_dev, 1), F32)
    for r in range(row_dev):
        own_counts = jnp.where(row == r, counts_ref[r].astype(F32), own_counts)
    omega = own_counts * rows / own_rows[:, 3:4]
    loss_ref[...] = jnp.broadcast_to(omega * own_rows[:, 2:3], loss_ref.shape)

    def core_copy(h):
        return pltpu.make_async_remote_copy(
            src_ref=part.at[h, pl.ds(pl.multiple_of((1 - core) * half, 8), half)],
            dst_ref=core_in.at[h],
            send_sem=core_send.at[h],
            recv_sem=core_recv.at[h],
            device_id={"blk": other},
            device_id_type=MESH,
        )

    def part_copy(h, k):
        target = lax.rem(chip + k, chips)
        return pltpu.make_async_remote_copy(
            src_ref=outbox.at[h, target],
            dst_ref=inbox.at[h, chip],
            send_sem=part_send.at[h, k],
            recv_sem=part_recv.at[h, chip],
            device_id={"blk": target * 2 + core},
            device_id_type=MESH,
        )

    def part_landed(h, k):
        slot = lax.rem(chip + k, chips)
        pltpu.make_async_remote_copy(
            src_ref=inbox.at[h, slot],
            dst_ref=inbox.at[h, slot],
            send_sem=part_send.at[h, k],
            recv_sem=part_recv.at[h, slot],
            device_id={"blk": other},
            device_id_type=MESH,
        ).wait_recv()

    def hand_on(h):
        core_copy(h).wait_recv()
        core_in[h] = core_in[h] + part[h, pl.ds(pl.multiple_of(core * half, 8), half), :]
        for d in range(chips):
            outbox[h, d] = core_in[h, pl.ds(d * row_dev, row_dev), :].astype(BF16)
        inbox[h, chip] = outbox[h, chip]
        loop(1, chips, lambda k: part_copy(h, k).start())

    for h in range(CUTS):
        for k in range(wide // strip):
            value = early[k] if h == 0 else raw(h, k)
            part[h, :, pl.ds(k * strip, strip)] = scaled(value, scale_s, scale_p)
        core_copy(h).start()
        if h:
            hand_on(h - 1)
    hand_on(CUTS - 1)

    for h in range(CUTS):
        loop(1, chips, lambda k: part_landed(h, k))
        total = jnp.zeros((row_dev, wide), F32)
        for d in range(chips):
            total = total + inbox[h, d].astype(F32)
        grad_ref[:, pl.ds(h * wide, wide)] = (total * omega).astype(BF16)

    def drain(k):
        for which in range(2):
            own_copy(which, k).wait_send()
            pair_copy(which, k).wait_send()
        for h in range(CUTS):
            part_copy(h, k).wait_send()

    loop(1, chips, drain)
    for which in range(2):
        pair_copy(which, 0).wait_send()
    for h in range(CUTS):
        core_copy(h).wait_send()
    loop(1, n, lambda k: stat_copy(k).wait_send())


def finish(loss_in, grad_in, loss_ref, grad_ref):
    for r in range(loss_ref.shape[0]):
        loss_ref[r] = loss_in[r, 0]
    grad_ref[...] = grad_in[...]


def on_device(n, student_hidden, teacher_hidden, counts, student_head, teacher_head):
    row_dev, ds = student_hidden.shape
    dt = teacher_hidden.shape[2]
    vocab = student_head.shape[1]
    rows = n * row_dev
    half = rows // 2
    chips = n // 2
    padded = -(-rows // 128) * 128
    wide = ds // CUTS
    dma = pltpu.SemaphoreType.DMA
    loss, grad = pl.pallas_call(
        functools.partial(kernel, n),
        out_shape=(
            jax.ShapeDtypeStruct((row_dev, 128), F32),
            jax.ShapeDtypeStruct((row_dev, ds), BF16),
        ),
        in_specs=[
            pl.BlockSpec(memory_space=pltpu.SMEM),
            pl.BlockSpec(memory_space=pltpu.VMEM),
            pl.BlockSpec(memory_space=pltpu.VMEM),
            pl.BlockSpec(memory_space=pl.ANY),
            pl.BlockSpec(memory_space=pl.ANY),
        ],
        out_specs=(
            pl.BlockSpec(memory_space=pltpu.VMEM),
            pl.BlockSpec(memory_space=pltpu.VMEM),
        ),
        scratch_shapes=[
            pltpu.VMEM((2, chips, row_dev, ds), BF16),
            pltpu.VMEM((2, chips, row_dev, dt), BF16),
            pltpu.VMEM((rows, ds), F32),
            pltpu.VMEM((rows, dt), F32),
            pltpu.VMEM((ds, vocab), BF16),
            pltpu.VMEM((dt, vocab), BF16),
            pltpu.VMEM((CUTS, rows, wide), F32),
            pltpu.VMEM((CUTS, half, wide), F32),
            pltpu.VMEM((CUTS, chips, row_dev, wide), BF16),
            pltpu.VMEM((CUTS, chips, row_dev, wide), BF16),
            pltpu.VMEM((n, 8, padded), F32),
            pltpu.VMEM((padded, 128), F32),
            dma((2,)),
            dma((2, chips)),
            dma((2, chips)),
            dma((2, chips)),
            dma((2, chips)),
            dma((n,)),
            dma((n,)),
            dma((CUTS,)),
            dma((CUTS,)),
            dma((CUTS, chips)),
            dma((CUTS, chips)),
        ],
        compiler_params=pltpu.CompilerParams(
            collective_id=0, has_side_effects=True, vmem_limit_bytes=56 * 1024 * 1024
        ),
    )(counts, student_hidden, teacher_hidden.reshape(row_dev, dt), student_head, teacher_head.reshape(dt, vocab))
    loss, grad = pl.pallas_call(
        finish,
        out_shape=(
            jax.ShapeDtypeStruct((row_dev,), F32),
            jax.ShapeDtypeStruct((row_dev, ds), BF16),
        ),
        in_specs=[
            pl.BlockSpec(memory_space=pltpu.SMEM),
            pl.BlockSpec(memory_space=pltpu.VMEM),
        ],
        out_specs=(
            pl.BlockSpec(memory_space=pltpu.SMEM),
            pl.BlockSpec(memory_space=pltpu.VMEM),
        ),
    )(loss, grad)
    return loss, grad


def solution(mesh):
    return jax.shard_map(
        functools.partial(on_device, mesh.shape["blk"]),
        mesh=mesh,
        in_specs=(
            P(("group", "blk"), None),
            P(("group", "blk"), None, None),
            P(("group", "blk")),
            P("group", "blk"),
            P(None, "group", "blk"),
        ),
        out_specs=(P(("group", "blk")), P(("group", "blk"), None)),
        check_vma=False,
    )
```

```python
import functools

import jax
import jax.numpy as jnp
from jax import lax
from jax.experimental import pallas as pl
from jax.experimental.pallas import tpu as pltpu
from jax.sharding import PartitionSpec as P

MESH = pl.DeviceIdType.MESH
F32 = jnp.float32
BF16 = jnp.bfloat16
CUTS = 1
STEPS = 4


def kernel(
    n, counts_ref, sh_ref, th_ref, sw_ref, tw_ref, loss_ref, grad_ref,
    sheld, theld, xs, xt, sw, tw, part, core_in, outbox, inbox, stats, table,
    w_sem, send_sem, recv_sem, pair_send, pair_recv, stat_send, stat_recv,
    core_send, core_recv, part_send, part_recv,
):
    row_dev, ds = sh_ref.shape
    dt = th_ref.shape[1]
    rows = n * row_dev
    half = rows // 2
    chips = n // 2
    me = lax.axis_index("blk")
    core = lax.rem(me, 2)
    chip = me // 2
    other = me + 1 - 2 * core
    wide = ds // CUTS

    weights = []
    for which, (src, dst) in enumerate(((sw_ref, sw), (tw_ref, tw))):
        copy = pltpu.make_async_copy(src, dst, w_sem.at[which])
        copy.start()
        weights.append(copy)

    barrier = pltpu.get_barrier_semaphore()

    def greet(k, carry):
        pl.semaphore_signal(
            barrier, inc=1, device_id={"blk": lax.rem(me + k, n)}, device_id_type=MESH
        )
        return carry

    lax.fori_loop(1, n, greet, 0)
    pl.semaphore_wait(barrier, n - 1)

    owns = (sh_ref, th_ref)
    helds = (sheld, theld)

    def own_copy(which, k):
        return pltpu.make_async_remote_copy(
            src_ref=owns[which],
            dst_ref=helds[which].at[core, chip],
            send_sem=send_sem.at[which, k],
            recv_sem=recv_sem.at[which, chip],
            device_id={"blk": lax.rem(chip + k, chips) * 2 + core},
            device_id_type=MESH,
        )

    def pair_copy(which, k):
        slot = lax.rem(chip - k + chips, chips)
        return pltpu.make_async_remote_copy(
            src_ref=owns[which] if isinstance(k, int) and k == 0 else helds[which].at[core, slot],
            dst_ref=helds[which].at[core, slot],
            send_sem=pair_send.at[which, slot],
            recv_sem=pair_recv.at[which, slot],
            device_id={"blk": other},
            device_id_type=MESH,
        )

    def landed(which, k):
        slot = lax.rem(chip - k + chips, chips)
        pltpu.make_async_remote_copy(
            src_ref=helds[which].at[core, slot],
            dst_ref=helds[which].at[core, slot],
            send_sem=send_sem.at[which, 0],
            recv_sem=recv_sem.at[which, slot],
            device_id={"blk": other},
            device_id_type=MESH,
        ).wait_recv()

    def pair_landed(which, k):
        slot = lax.rem(chip - k + chips, chips)
        pltpu.make_async_remote_copy(
            src_ref=helds[which].at[1 - core, slot],
            dst_ref=helds[which].at[1 - core, slot],
            send_sem=send_sem.at[which, 0],
            recv_sem=pair_recv.at[which, slot],
            device_id={"blk": other},
            device_id_type=MESH,
        ).wait_recv()

    def loop(low, high, body):
        if high - low <= 16:
            for k in range(low, high):
                body(k)
        else:
            lax.fori_loop(low, high, lambda k, carry: (body(k), carry)[1], 0)

    for which in range(2):
        loop(1, chips, lambda k, which=which: own_copy(which, k).start())
        pair_copy(which, 0).start()

    def pass_on(which, k):
        landed(which, k)
        pair_copy(which, k).start()

    def settle(which, x):
        loop(0, chips, lambda k: pair_landed(which, k))
        for c in range(2):
            for d in range(chips):
                x[pl.ds(c * half + d * row_dev, row_dev), :] = helds[which][c, d].astype(F32)

    def term(x, w, k, total):
        cut = w.shape[0] // STEPS
        at = pl.ds(k * cut, cut)
        return total + jnp.dot(x[:, at].astype(BF16), w[at, :], preferred_element_type=F32)

    sheld[core, chip] = sh_ref[...]
    theld[core, chip] = th_ref[...]
    loop(1, chips, lambda k: pass_on(0, k))
    settle(0, xs)
    weights[0].wait()
    student = jnp.zeros((rows, sw.shape[1]), F32)
    share = -(-(chips - 1) // STEPS)
    for k in range(STEPS):
        student = term(xs, sw, k, student)
        loop(
            1 + k * share, max(1 + k * share, min(chips, 1 + (k + 1) * share)),
            lambda j: pass_on(1, j),
        )
    peak_s = jnp.max(student, axis=1, keepdims=True)
    exp_s = jnp.exp(student - peak_s)
    sum_s = jnp.sum(exp_s, axis=1, keepdims=True)
    settle(1, xt)
    weights[1].wait()
    score = jnp.zeros((rows, tw.shape[1]), F32)
    for k in range(STEPS):
        score = term(xt, tw, k, score)

    peak_p = jnp.max(score, axis=1, keepdims=True)
    exp_p = jnp.exp(score - peak_p)
    sum_p = jnp.sum(exp_p, axis=1, keepdims=True)
    weighted = jnp.sum(exp_p * (score - student), axis=1, keepdims=True)
    own_count = counts_ref[0]
    for r in range(1, row_dev):
        own_count = own_count + counts_ref[r]
    padded = table.shape[0]
    lane = lax.broadcasted_iota(jnp.int32, (rows, 128), 1)
    packed = jnp.where(lane == 5, own_count.astype(F32), 0.0)
    for k, column in enumerate((peak_s, sum_s, peak_p, sum_p, weighted)):
        packed = jnp.where(lane == k, column, packed)
    table[pl.ds(0, rows), :] = packed
    if padded > rows:
        table[pl.ds(rows, padded - rows), :] = jnp.zeros((padded - rows, 128), F32)
    stats[me] = jnp.transpose(table[...])[:8, :]

    def stat_copy(k):
        return pltpu.make_async_remote_copy(
            src_ref=stats.at[me],
            dst_ref=stats.at[me],
            send_sem=stat_send.at[k],
            recv_sem=stat_recv.at[me],
            device_id={"blk": lax.rem(me + k, n)},
            device_id_type=MESH,
        )

    def stat_landed(k):
        slot = lax.rem(me + k, n)
        pltpu.make_async_remote_copy(
            src_ref=stats.at[slot],
            dst_ref=stats.at[slot],
            send_sem=stat_send.at[k],
            recv_sem=stat_recv.at[slot],
            device_id={"blk": other},
            device_id_type=MESH,
        ).wait_recv()

    loop(1, n, lambda k: stat_copy(k).start())

    high_s = exp_s.astype(BF16)
    high_p = exp_p.astype(BF16)
    low_s = (exp_s - high_s.astype(F32)).astype(BF16)
    low_p = (exp_p - high_p.astype(F32)).astype(BF16)
    stacked = jnp.concatenate([high_s, low_s, high_p, low_p], axis=0)
    strip = 512 if wide % 512 == 0 else wide

    def raw(h, k):
        return lax.dot_general(
            stacked, sw[pl.ds(h * wide + k * strip, strip), :], (((1,), (1,)), ((), ())),
            preferred_element_type=F32,
        )

    def core_copy(h):
        return pltpu.make_async_remote_copy(
            src_ref=part.at[h, :, pl.ds(pl.multiple_of((1 - core) * half, 8), half)],
            dst_ref=core_in.at[h],
            send_sem=core_send.at[h],
            recv_sem=core_recv.at[h],
            device_id={"blk": other},
            device_id_type=MESH,
        )

    for h in range(CUTS):
        for k in range(wide // strip):
            value = raw(h, k)
            for m in range(2):
                part[h, m, :, pl.ds(k * strip, strip)] = (
                    value[2 * m * rows:(2 * m + 1) * rows]
                    + value[(2 * m + 1) * rows:(2 * m + 2) * rows]
                )
        core_copy(h).start()
    loop(1, n, stat_landed)

    all_stats = stats[...]
    top_s = jnp.max(all_stats[:, 0:1, :], axis=0)
    top_p = jnp.max(all_stats[:, 2:3, :], axis=0)
    change_p = jnp.exp(all_stats[:, 2:3, :] - top_p[None])
    total_s = jnp.sum(jnp.exp(all_stats[:, 0:1, :] - top_s[None]) * all_stats[:, 1:2, :], axis=0)
    total_p = jnp.sum(change_p * all_stats[:, 3:4, :], axis=0)
    total_w = jnp.sum(change_p * all_stats[:, 4:5, :], axis=0)
    total_count = jnp.sum(all_stats[:, 5:6, :], axis=0)
    lse_s = top_s + jnp.log(total_s)
    lse_p = top_p + jnp.log(total_p)
    divergence = total_w / total_p - lse_p + lse_s
    line = lax.broadcasted_iota(jnp.int32, (128, padded), 0)
    merged = jnp.where(line == 0, lse_s, 0.0)
    merged = jnp.where(line == 1, lse_p, merged)
    merged = jnp.where(line == 2, divergence, merged)
    merged = jnp.where(line == 3, total_count, merged)
    for k, device in enumerate((me, other)):
        merged = jnp.where(line == 4 + 2 * k, jnp.exp(stats[device, 0:1, :] - lse_s), merged)
        merged = jnp.where(line == 5 + 2 * k, jnp.exp(stats[device, 2:3, :] - lse_p), merged)
    table[...] = jnp.transpose(merged)
    kept = pl.ds(pl.multiple_of(core * half, 8), half)
    scales = table[kept, :]

    own_rows = table[pl.ds(core * half + chip * row_dev, row_dev), :]
    row = lax.broadcasted_iota(jnp.int32, (row_dev, 1), 0)
    own_counts = jnp.zeros((row_dev, 1), F32)
    for r in range(row_dev):
        own_counts = jnp.where(row == r, counts_ref[r].astype(F32), own_counts)
    omega = own_counts * rows / own_rows[:, 3:4]
    loss_ref[...] = jnp.broadcast_to(omega * own_rows[:, 2:3], loss_ref.shape)

    def part_copy(h, k):
        target = lax.rem(chip + k, chips)
        return pltpu.make_async_remote_copy(
            src_ref=outbox.at[h, target],
            dst_ref=inbox.at[h, chip],
            send_sem=part_send.at[h, k],
            recv_sem=part_recv.at[h, chip],
            device_id={"blk": target * 2 + core},
            device_id_type=MESH,
        )

    def part_landed(h, k):
        slot = lax.rem(chip + k, chips)
        pltpu.make_async_remote_copy(
            src_ref=inbox.at[h, slot],
            dst_ref=inbox.at[h, slot],
            send_sem=part_send.at[h, k],
            recv_sem=part_recv.at[h, slot],
            device_id={"blk": other},
            device_id_type=MESH,
        ).wait_recv()

    for h in range(CUTS):
        core_copy(h).wait_recv()
        total = scales[:, 4:5] * part[h, 0, kept, :] - scales[:, 5:6] * part[h, 1, kept, :]
        core_in[h, 0] = total + (
            scales[:, 6:7] * core_in[h, 0] - scales[:, 7:8] * core_in[h, 1]
        )
        for d in range(chips):
            outbox[h, d] = core_in[h, 0, pl.ds(d * row_dev, row_dev), :].astype(BF16)
        inbox[h, chip] = outbox[h, chip]
        loop(1, chips, lambda k: part_copy(h, k).start())

    for h in range(CUTS):
        loop(1, chips, lambda k: part_landed(h, k))
        total = jnp.zeros((row_dev, wide), F32)
        for d in range(chips):
            total = total + inbox[h, d].astype(F32)
        grad_ref[:, pl.ds(h * wide, wide)] = (total * omega).astype(BF16)

    def drain(k):
        for which in range(2):
            own_copy(which, k).wait_send()
            pair_copy(which, k).wait_send()
        for h in range(CUTS):
            part_copy(h, k).wait_send()

    loop(1, chips, drain)
    for which in range(2):
        pair_copy(which, 0).wait_send()
    for h in range(CUTS):
        core_copy(h).wait_send()
    loop(1, n, lambda k: stat_copy(k).wait_send())


def finish(loss_in, grad_in, loss_ref, grad_ref):
    for r in range(loss_ref.shape[0]):
        loss_ref[r] = loss_in[r, 0]
    grad_ref[...] = grad_in[...]


def on_device(n, student_hidden, teacher_hidden, counts, student_head, teacher_head):
    row_dev, ds = student_hidden.shape
    dt = teacher_hidden.shape[2]
    vocab = student_head.shape[1]
    rows = n * row_dev
    half = rows // 2
    chips = n // 2
    padded = -(-rows // 128) * 128
    wide = ds // CUTS
    dma = pltpu.SemaphoreType.DMA
    loss, grad = pl.pallas_call(
        functools.partial(kernel, n),
        out_shape=(
            jax.ShapeDtypeStruct((row_dev, 128), F32),
            jax.ShapeDtypeStruct((row_dev, ds), BF16),
        ),
        in_specs=[
            pl.BlockSpec(memory_space=pltpu.SMEM),
            pl.BlockSpec(memory_space=pltpu.VMEM),
            pl.BlockSpec(memory_space=pltpu.VMEM),
            pl.BlockSpec(memory_space=pl.ANY),
            pl.BlockSpec(memory_space=pl.ANY),
        ],
        out_specs=(
            pl.BlockSpec(memory_space=pltpu.VMEM),
            pl.BlockSpec(memory_space=pltpu.VMEM),
        ),
        scratch_shapes=[
            pltpu.VMEM((2, chips, row_dev, ds), BF16),
            pltpu.VMEM((2, chips, row_dev, dt), BF16),
            pltpu.VMEM((rows, ds), F32),
            pltpu.VMEM((rows, dt), F32),
            pltpu.VMEM((ds, vocab), BF16),
            pltpu.VMEM((dt, vocab), BF16),
            pltpu.VMEM((CUTS, 2, rows, wide), F32),
            pltpu.VMEM((CUTS, 2, half, wide), F32),
            pltpu.VMEM((CUTS, chips, row_dev, wide), BF16),
            pltpu.VMEM((CUTS, chips, row_dev, wide), BF16),
            pltpu.VMEM((n, 8, padded), F32),
            pltpu.VMEM((padded, 128), F32),
            dma((2,)),
            dma((2, chips)),
            dma((2, chips)),
            dma((2, chips)),
            dma((2, chips)),
            dma((n,)),
            dma((n,)),
            dma((CUTS,)),
            dma((CUTS,)),
            dma((CUTS, chips)),
            dma((CUTS, chips)),
        ],
        compiler_params=pltpu.CompilerParams(
            collective_id=0, has_side_effects=True, vmem_limit_bytes=56 * 1024 * 1024
        ),
    )(counts, student_hidden, teacher_hidden.reshape(row_dev, dt), student_head, teacher_head.reshape(dt, vocab))
    loss, grad = pl.pallas_call(
        finish,
        out_shape=(
            jax.ShapeDtypeStruct((row_dev,), F32),
            jax.ShapeDtypeStruct((row_dev, ds), BF16),
        ),
        in_specs=[
            pl.BlockSpec(memory_space=pltpu.SMEM),
            pl.BlockSpec(memory_space=pltpu.VMEM),
        ],
        out_specs=(
            pl.BlockSpec(memory_space=pltpu.SMEM),
            pl.BlockSpec(memory_space=pltpu.VMEM),
        ),
    )(loss, grad)
    return loss, grad


def solution(mesh):
    return jax.shard_map(
        functools.partial(on_device, mesh.shape["blk"]),
        mesh=mesh,
        in_specs=(
            P(("group", "blk"), None),
            P(("group", "blk"), None, None),
            P(("group", "blk")),
            P("group", "blk"),
            P(None, "group", "blk"),
        ),
        out_specs=(P(("group", "blk")), P(("group", "blk"), None)),
        check_vma=False,
    )
```

```python
import functools

import jax
import jax.numpy as jnp
from jax import lax
from jax.experimental import pallas as pl
from jax.experimental.pallas import tpu as pltpu
from jax.sharding import PartitionSpec as P

MESH = pl.DeviceIdType.MESH
F32 = jnp.float32
BF16 = jnp.bfloat16
CUTS = 1
STEPS = 4


def kernel(
    n, counts_ref, sh_ref, th_ref, sw_ref, tw_ref, loss_ref, grad_ref,
    sheld, theld, xs, xt, sw, tw, part, core_in, outbox, inbox, stats, table,
    w_sem, send_sem, recv_sem, pair_send, pair_recv, stat_send, stat_recv,
    core_send, core_recv, part_send, part_recv,
):
    row_dev, ds = sh_ref.shape
    dt = th_ref.shape[1]
    rows = n * row_dev
    half = rows // 2
    chips = n // 2
    me = lax.axis_index("blk")
    core = lax.rem(me, 2)
    chip = me // 2
    other = me + 1 - 2 * core
    wide = ds // CUTS

    weights = []
    for which, (src, dst) in enumerate(((sw_ref, sw), (tw_ref, tw))):
        copy = pltpu.make_async_copy(src, dst, w_sem.at[which])
        copy.start()
        weights.append(copy)

    barrier = pltpu.get_barrier_semaphore()

    def greet(k, carry):
        pl.semaphore_signal(
            barrier, inc=1, device_id={"blk": lax.rem(me + k, n)}, device_id_type=MESH
        )
        return carry

    lax.fori_loop(1, n, greet, 0)
    pl.semaphore_wait(barrier, n - 1)

    owns = (sh_ref, th_ref)
    helds = (sheld, theld)

    def own_copy(which, k):
        return pltpu.make_async_remote_copy(
            src_ref=owns[which],
            dst_ref=helds[which].at[core, chip],
            send_sem=send_sem.at[which, k],
            recv_sem=recv_sem.at[which, chip],
            device_id={"blk": lax.rem(chip + k, chips) * 2 + core},
            device_id_type=MESH,
        )

    def pair_copy(which, k):
        slot = lax.rem(chip - k + chips, chips)
        return pltpu.make_async_remote_copy(
            src_ref=owns[which] if isinstance(k, int) and k == 0 else helds[which].at[core, slot],
            dst_ref=helds[which].at[core, slot],
            send_sem=pair_send.at[which, slot],
            recv_sem=pair_recv.at[which, slot],
            device_id={"blk": other},
            device_id_type=MESH,
        )

    def landed(which, k):
        slot = lax.rem(chip - k + chips, chips)
        pltpu.make_async_remote_copy(
            src_ref=helds[which].at[core, slot],
            dst_ref=helds[which].at[core, slot],
            send_sem=send_sem.at[which, 0],
            recv_sem=recv_sem.at[which, slot],
            device_id={"blk": other},
            device_id_type=MESH,
        ).wait_recv()

    def pair_landed(which, k):
        slot = lax.rem(chip - k + chips, chips)
        pltpu.make_async_remote_copy(
            src_ref=helds[which].at[1 - core, slot],
            dst_ref=helds[which].at[1 - core, slot],
            send_sem=send_sem.at[which, 0],
            recv_sem=pair_recv.at[which, slot],
            device_id={"blk": other},
            device_id_type=MESH,
        ).wait_recv()

    def loop(low, high, body):
        if high - low <= 16:
            for k in range(low, high):
                body(k)
        else:
            lax.fori_loop(low, high, lambda k, carry: (body(k), carry)[1], 0)

    for which in range(2):
        loop(1, chips, lambda k, which=which: own_copy(which, k).start())
        pair_copy(which, 0).start()

    def pass_on(which, k):
        landed(which, k)
        pair_copy(which, k).start()

    def settle(which, x):
        loop(0, chips, lambda k: pair_landed(which, k))
        for c in range(2):
            for d in range(chips):
                x[pl.ds(c * half + d * row_dev, row_dev), :] = helds[which][c, d].astype(F32)

    def term(x, w, k, total):
        cut = w.shape[0] // STEPS
        at = pl.ds(k * cut, cut)
        return total + jnp.dot(x[:, at].astype(BF16), w[at, :], preferred_element_type=F32)

    sheld[core, chip] = sh_ref[...]
    theld[core, chip] = th_ref[...]
    loop(1, chips, lambda k: pass_on(0, k))
    settle(0, xs)
    weights[0].wait()
    student = jnp.zeros((rows, sw.shape[1]), F32)
    share = -(-(chips - 1) // STEPS)
    for k in range(STEPS):
        student = term(xs, sw, k, student)
        loop(
            1 + k * share, max(1 + k * share, min(chips, 1 + (k + 1) * share)),
            lambda j: pass_on(1, j),
        )
    peak_s = jnp.max(student, axis=1, keepdims=True)
    exp_s = jnp.exp(student - peak_s)
    sum_s = jnp.sum(exp_s, axis=1, keepdims=True)
    settle(1, xt)
    weights[1].wait()
    score = jnp.zeros((rows, tw.shape[1]), F32)
    for k in range(STEPS):
        score = term(xt, tw, k, score)

    peak_p = jnp.max(score, axis=1, keepdims=True)
    exp_p = jnp.exp(score - peak_p)
    sum_p = jnp.sum(exp_p, axis=1, keepdims=True)
    weighted = jnp.sum(exp_p * (score - student), axis=1, keepdims=True)
    own_count = counts_ref[0]
    for r in range(1, row_dev):
        own_count = own_count + counts_ref[r]
    padded = table.shape[0]
    lane = lax.broadcasted_iota(jnp.int32, (rows, 128), 1)
    packed = jnp.where(lane == 5, own_count.astype(F32), 0.0)
    for k, column in enumerate((peak_s, sum_s, peak_p, sum_p, weighted)):
        packed = jnp.where(lane == k, column, packed)
    table[pl.ds(0, rows), :] = packed
    if padded > rows:
        table[pl.ds(rows, padded - rows), :] = jnp.zeros((padded - rows, 128), F32)
    stats[me] = jnp.transpose(table[...])[:8, :]

    def stat_copy(k):
        return pltpu.make_async_remote_copy(
            src_ref=stats.at[me],
            dst_ref=stats.at[me],
            send_sem=stat_send.at[k],
            recv_sem=stat_recv.at[me],
            device_id={"blk": lax.rem(me + k, n)},
            device_id_type=MESH,
        )

    def stat_landed(k):
        slot = lax.rem(me + k, n)
        pltpu.make_async_remote_copy(
            src_ref=stats.at[slot],
            dst_ref=stats.at[slot],
            send_sem=stat_send.at[k],
            recv_sem=stat_recv.at[slot],
            device_id={"blk": other},
            device_id_type=MESH,
        ).wait_recv()

    loop(1, n, lambda k: stat_copy(k).start())

    high_s = exp_s.astype(BF16)
    high_p = exp_p.astype(BF16)
    low_s = (exp_s - high_s.astype(F32)).astype(BF16)
    low_p = (exp_p - high_p.astype(F32)).astype(BF16)
    stacked = jnp.concatenate([high_s, low_s, high_p, low_p], axis=0)
    strip = 512 if wide % 512 == 0 else wide

    def raw(h, k):
        return lax.dot_general(
            stacked, sw[pl.ds(h * wide + k * strip, strip), :], (((1,), (1,)), ((), ())),
            preferred_element_type=F32,
        )

    def core_copy(h):
        return pltpu.make_async_remote_copy(
            src_ref=part.at[h, :, pl.ds(pl.multiple_of((1 - core) * half, 8), half)],
            dst_ref=core_in.at[h],
            send_sem=core_send.at[h],
            recv_sem=core_recv.at[h],
            device_id={"blk": other},
            device_id_type=MESH,
        )

    for h in range(CUTS):
        for k in range(wide // strip):
            value = raw(h, k)
            for m in range(2):
                part[h, m, :, pl.ds(k * strip, strip)] = (
                    value[2 * m * rows:(2 * m + 1) * rows]
                    + value[(2 * m + 1) * rows:(2 * m + 2) * rows]
                )
        core_copy(h).start()
    loop(1, n, stat_landed)

    all_stats = stats[...]
    top_s = jnp.max(all_stats[:, 0:1, :], axis=0)
    top_p = jnp.max(all_stats[:, 2:3, :], axis=0)
    change_p = jnp.exp(all_stats[:, 2:3, :] - top_p[None])
    total_s = jnp.sum(jnp.exp(all_stats[:, 0:1, :] - top_s[None]) * all_stats[:, 1:2, :], axis=0)
    total_p = jnp.sum(change_p * all_stats[:, 3:4, :], axis=0)
    total_w = jnp.sum(change_p * all_stats[:, 4:5, :], axis=0)
    total_count = jnp.sum(all_stats[:, 5:6, :], axis=0)
    lse_s = top_s + jnp.log(total_s)
    lse_p = top_p + jnp.log(total_p)
    divergence = total_w / total_p - lse_p + lse_s
    line = lax.broadcasted_iota(jnp.int32, (128, padded), 0)
    merged = jnp.where(line == 0, lse_s, 0.0)
    merged = jnp.where(line == 1, lse_p, merged)
    merged = jnp.where(line == 2, divergence, merged)
    merged = jnp.where(line == 3, total_count, merged)
    for k, device in enumerate((me, other)):
        merged = jnp.where(line == 4 + 2 * k, jnp.exp(stats[device, 0:1, :] - lse_s), merged)
        merged = jnp.where(line == 5 + 2 * k, jnp.exp(stats[device, 2:3, :] - lse_p), merged)
    table[...] = jnp.transpose(merged)
    kept = pl.ds(pl.multiple_of(core * half, 8), half)
    scales = table[kept, :]

    own_rows = table[pl.ds(core * half + chip * row_dev, row_dev), :]
    row = lax.broadcasted_iota(jnp.int32, (row_dev, 1), 0)
    own_counts = jnp.zeros((row_dev, 1), F32)
    for r in range(row_dev):
        own_counts = jnp.where(row == r, counts_ref[r].astype(F32), own_counts)
    omega = own_counts * rows / own_rows[:, 3:4]
    loss_ref[...] = jnp.broadcast_to(omega * own_rows[:, 2:3], loss_ref.shape)

    def part_copy(h, k):
        target = lax.rem(chip + k, chips)
        return pltpu.make_async_remote_copy(
            src_ref=outbox.at[h, target],
            dst_ref=inbox.at[h, chip],
            send_sem=part_send.at[h, target],
            recv_sem=part_recv.at[h, chip],
            device_id={"blk": target * 2 + core},
            device_id_type=MESH,
        )

    def part_landed(h, k):
        slot = lax.rem(chip + k, chips)
        pltpu.make_async_remote_copy(
            src_ref=inbox.at[h, slot],
            dst_ref=inbox.at[h, slot],
            send_sem=part_send.at[h, k],
            recv_sem=part_recv.at[h, slot],
            device_id={"blk": other},
            device_id_type=MESH,
        ).wait_recv()

    for h in range(CUTS):
        core_copy(h).wait_recv()
        total = scales[:, 4:5] * part[h, 0, kept, :] - scales[:, 5:6] * part[h, 1, kept, :]
        core_in[h, 0] = total + (
            scales[:, 6:7] * core_in[h, 0] - scales[:, 7:8] * core_in[h, 1]
        )
        for d in range(chips):
            outbox[h, d] = core_in[h, 0, pl.ds(d * row_dev, row_dev), :].astype(BF16)

            @pl.when(chip != d)
            def _():
                part_copy(h, d - chip + chips).start()

        inbox[h, chip] = outbox[h, chip]

    for h in range(CUTS):
        loop(1, chips, lambda k: part_landed(h, k))
        total = jnp.zeros((row_dev, wide), F32)
        for d in range(chips):
            total = total + inbox[h, d].astype(F32)
        grad_ref[:, pl.ds(h * wide, wide)] = (total * omega).astype(BF16)

    def drain(k):
        for which in range(2):
            own_copy(which, k).wait_send()
            pair_copy(which, k).wait_send()
        for h in range(CUTS):
            part_copy(h, k).wait_send()

    loop(1, chips, drain)
    for which in range(2):
        pair_copy(which, 0).wait_send()
    for h in range(CUTS):
        core_copy(h).wait_send()
    loop(1, n, lambda k: stat_copy(k).wait_send())


def finish(loss_in, grad_in, loss_ref, grad_ref):
    for r in range(loss_ref.shape[0]):
        loss_ref[r] = loss_in[r, 0]
    grad_ref[...] = grad_in[...]


def on_device(n, student_hidden, teacher_hidden, counts, student_head, teacher_head):
    row_dev, ds = student_hidden.shape
    dt = teacher_hidden.shape[2]
    vocab = student_head.shape[1]
    rows = n * row_dev
    half = rows // 2
    chips = n // 2
    padded = -(-rows // 128) * 128
    wide = ds // CUTS
    dma = pltpu.SemaphoreType.DMA
    loss, grad = pl.pallas_call(
        functools.partial(kernel, n),
        out_shape=(
            jax.ShapeDtypeStruct((row_dev, 128), F32),
            jax.ShapeDtypeStruct((row_dev, ds), BF16),
        ),
        in_specs=[
            pl.BlockSpec(memory_space=pltpu.SMEM),
            pl.BlockSpec(memory_space=pltpu.VMEM),
            pl.BlockSpec(memory_space=pltpu.VMEM),
            pl.BlockSpec(memory_space=pl.ANY),
            pl.BlockSpec(memory_space=pl.ANY),
        ],
        out_specs=(
            pl.BlockSpec(memory_space=pltpu.VMEM),
            pl.BlockSpec(memory_space=pltpu.VMEM),
        ),
        scratch_shapes=[
            pltpu.VMEM((2, chips, row_dev, ds), BF16),
            pltpu.VMEM((2, chips, row_dev, dt), BF16),
            pltpu.VMEM((rows, ds), F32),
            pltpu.VMEM((rows, dt), F32),
            pltpu.VMEM((ds, vocab), BF16),
            pltpu.VMEM((dt, vocab), BF16),
            pltpu.VMEM((CUTS, 2, rows, wide), F32),
            pltpu.VMEM((CUTS, 2, half, wide), F32),
            pltpu.VMEM((CUTS, chips, row_dev, wide), BF16),
            pltpu.VMEM((CUTS, chips, row_dev, wide), BF16),
            pltpu.VMEM((n, 8, padded), F32),
            pltpu.VMEM((padded, 128), F32),
            dma((2,)),
            dma((2, chips)),
            dma((2, chips)),
            dma((2, chips)),
            dma((2, chips)),
            dma((n,)),
            dma((n,)),
            dma((CUTS,)),
            dma((CUTS,)),
            dma((CUTS, chips)),
            dma((CUTS, chips)),
        ],
        compiler_params=pltpu.CompilerParams(
            collective_id=0, has_side_effects=True, vmem_limit_bytes=56 * 1024 * 1024
        ),
    )(counts, student_hidden, teacher_hidden.reshape(row_dev, dt), student_head, teacher_head.reshape(dt, vocab))
    loss, grad = pl.pallas_call(
        finish,
        out_shape=(
            jax.ShapeDtypeStruct((row_dev,), F32),
            jax.ShapeDtypeStruct((row_dev, ds), BF16),
        ),
        in_specs=[
            pl.BlockSpec(memory_space=pltpu.SMEM),
            pl.BlockSpec(memory_space=pltpu.VMEM),
        ],
        out_specs=(
            pl.BlockSpec(memory_space=pltpu.SMEM),
            pl.BlockSpec(memory_space=pltpu.VMEM),
        ),
    )(loss, grad)
    return loss, grad


def solution(mesh):
    return jax.shard_map(
        functools.partial(on_device, mesh.shape["blk"]),
        mesh=mesh,
        in_specs=(
            P(("group", "blk"), None),
            P(("group", "blk"), None, None),
            P(("group", "blk")),
            P("group", "blk"),
            P(None, "group", "blk"),
        ),
        out_specs=(P(("group", "blk")), P(("group", "blk"), None)),
        check_vma=False,
    )
```
